768 devices in a mesh: row: 32 (over z_hi, x, core), col: 24 (over z_lo, y).
Axes of the slice: x: 4, y: 8, z: 12 (z_hi: 4, z_lo: 3; z = z_hi * 3 + z_lo), core: 2. Of those that a mesh axis runs over, the one named last changes fastest.
Arguments:
- inverse_tiles: float32 [12288, 12288], P('row', 'col'), may hold values from -0.078125 to 0.078125
- factor_panels: float32 [3, 512, 6144], P(None, 'row', 'col'), may hold values from -6 to 6
- block_rows: int32 [3, 192], replicated, may hold values from 0 to 383, as said below
- couplings: float32 [2, 512, 512], replicated, may hold values from -0.25 to 0.25
Outputs:
- new_columns: float32 [3, 12288, 512], P(None, ('row', 'col'))
The draws below stay inside these ranges and needn't reach their ends.
Inputs may be any that keep to these rules, and one draw needn't show every extreme that they name: `block_rows`: each row lists 192 different row blocks in no particular order; in each row, all 16 blocks q * 16 to q * 16 + 15 of some q are listed.
All inputs are finite; a program needn't handle non-finite values.
Results may differ from the reference program's by a relative error of at most 0.0001.
Values sent between devices are 32-bit elements; how exact they have to be, the bound alone decides.
A program may use at most 32 MiB of HBM per device.

```python
import jax
import jax.numpy as jnp
from jax import lax

W = 512
RB = 32
SUPERNODES = 3
M = 12288
NB = 384
NBC = 16
NZB = 192
NZ = 6144


def draw_block_rows(key, part):
    listed = []
    for section in range(SUPERNODES):
        branch = jax.random.fold_in(key, 11 + section)
        order = jax.random.permutation(jax.random.fold_in(branch, 1), NB).astype(jnp.int32)
        chosen = jax.random.randint(jax.random.fold_in(branch, 2), (), 0, NB // NBC)
        blocks = jnp.arange(NB, dtype=jnp.int32)
        scores = order + NB * (blocks // NBC == chosen).astype(jnp.int32)
        picked = lax.top_k(scores, NZB)[1].astype(jnp.int32)
        listed.append(jax.random.permutation(jax.random.fold_in(branch, 3), picked))
    return jnp.stack(listed).astype(jnp.int32)


def levels(own_key, shape, shards, least, top_value):
    loudness = 1.0
    for axis_at, blocks in shards:
        draws = jax.random.uniform(jax.random.fold_in(jax.random.fold_in(own_key, 6), axis_at), (blocks,), jnp.float32, least / len(shards), top_value / len(shards))
        loudness = loudness * jnp.repeat(jnp.exp(draws), shape[axis_at] // blocks).reshape((-1,) + (1,) * (len(shape) - 1 - axis_at))
    return loudness


def gaussian(key, extent, deviation, most, cuts=(), kind=jnp.bfloat16):
    array = deviation * jax.random.normal(key, extent, jnp.float32)
    if cuts:
        array = array * levels(key, extent, cuts, -0.22, 0.18)
    return jnp.clip(array, -most, most).astype(kind)


def setup_inputs(seed: int = 0) -> dict:
    key_of = jax.random.split(jax.random.key(seed), 5)
    return {
        "inverse_tiles": gaussian(key_of[0], (M, M), NZ ** -0.5, 0.078125, ((0, 32), (1, 24)), jnp.float32),
        "factor_panels": gaussian(key_of[1], (SUPERNODES, W, NZ), 1.0, 6.0, ((1, 32), (2, 24)), jnp.float32),
        "block_rows": draw_block_rows(jax.random.fold_in(key_of[4], 71), 0),
        "couplings": gaussian(key_of[3], (SUPERNODES - 1, W, W), W ** -0.5, 0.25, (), jnp.float32),
    }


def reference(inverse_tiles, factor_panels, block_rows, couplings):
    results = []
    previous = None
    for section in range(SUPERNODES):
        onehot = (block_rows[section][:, None] == jnp.arange(NB, dtype=jnp.int32)[None, :]).astype(jnp.float32)
        blocks = factor_panels[section].reshape(W, NZB, RB)
        full_t = jnp.einsum("wpr,pb->wbr", blocks, onehot, precision=lax.Precision.HIGHEST).reshape(W, M)
        product = lax.dot_general(inverse_tiles, full_t, (((1,), (1,)), ((), ())), precision=lax.Precision.HIGHEST, preferred_element_type=jnp.float32)
        if previous is not None:
            product = product + jnp.dot(previous, couplings[section - 1], precision=lax.Precision.HIGHEST, preferred_element_type=jnp.float32)
        previous = -product
        results.append(previous)
    return jnp.stack(results)
```

```python
import jax
import jax.numpy as jnp
from jax import lax
from jax.experimental import pallas as pl
from jax.experimental.pallas import tpu as pltpu
from jax.sharding import PartitionSpec as P

ZH, X, CORE, ZL, Y = 4, 4, 2, 3, 8
S, W, RB, NBC, NZB = 3, 512, 32, 16, 192
WP = W // (ZH * X * CORE)
LISTED = NZB // (ZL * Y)
ROWS, DEPTH = 384, 512
OUT = ROWS // (ZL * Y)
TARGETS = ZL * NBC
QUAD = 128 // RB
MESH = pl.DeviceIdType.MESH
F32, BF16 = jnp.float32, jnp.bfloat16
COPIES = 256
GROUPS = ((4,), (3, -3), (2, -2), (1, -1), (0,))
Z_FIRST = (2,)
ORDER = (
    (1, 0), (1, 1), (0,), (1, 2), (2, 0), (2, 1), (3, 0), (2, 2), (3, 1), (4, 0, 2), (3, 2), (4, 0, 3),
    (4, 0, 1), (5, 0, 0), (4, 1, 2), (4, 1, 3), (4, 1, 1), (5, 1, 0), (5, 0, 2), (5, 0, 1), (5, 0, -1),
    (4, 2, 2), (4, 2, 1), (4, 2, 3), (5, 2, 0), (6, 0), (5, 1, 2), (5, 1, 1), (5, 1, -1), (6, 1),
    (8, 0, 1, 0), (8, 0, 0, 0), (5, 2, 2), (8, 0, 2, 0), (5, 2, -1), (5, 2, 1), (6, 2), (8, 1, 1, 0),
    (8, 1, 0, 0), (8, 0, 1, 1), (8, 1, 2, 0), (8, 0, 0, 1), (8, 0, 2, 1), (7, 2, 0), (8, 1, 1, 1),
    (8, 1, 0, 1), (7, 2, 1), (8, 0, 1, 2), (8, 1, 2, 1), (7, 2, 2), (8, 0, 0, 2), (8, 0, 2, 2), (8, 2, 2, 0),
    (7, 2, 3), (8, 1, 1, 2), (7, 2, 4), (8, 1, 0, 2), (8, 0, 1, 3), (8, 1, 2, 2), (8, 0, 0, 3), (8, 0, 2, 3),
    (8, 2, 2, 1), (8, 1, 1, 3), (8, 1, 0, 3), (8, 1, 2, 3), (9, 0), (8, 2, 2, 2), (9, 1), (8, 2, 2, 3),
    (9, 2),
)


def split(value):
    high = value.astype(BF16)
    return high, (value - high.astype(F32)).astype(BF16)


def dot3(a_high, a_low, b_high, b_low, dims):
    def one(a, b):
        return lax.dot_general(a, b, (dims, ((), ())), preferred_element_type=F32)

    return one(a_high, b_high) + (one(a_high, b_low) + one(a_low, b_high))


def kernel(
    table, a_hbm, f_ref, k_hbm, o_ref,
    a_ref, k_ref, f_own, listed_0, listed_1, listed_2, picked, from_zl, factor, partial,
    half_in, step_in, whole_in, last_in, a_high, a_low, k_high, k_low, fill_sem, send_sem, recv_sem,
):
    row, col = lax.axis_index("row"), lax.axis_index("col")
    zh, x, core = row // (X * CORE), lax.rem(row // CORE, X), lax.rem(row, CORE)
    zl, y = col // Y, lax.rem(col, Y)
    listed = (listed_0, listed_1, listed_2)

    def turn(value, by, size):
        return lax.rem(value + (by + size), size)

    def device(dzh=0, dx=0, dcore=0, dzl=0, dy=0):
        at_row = (turn(zh, dzh, ZH) * X + turn(x, dx, X)) * CORE + (1 - core if dcore else core)
        return (at_row, turn(zl, dzl, ZL) * Y + turn(y, dy, Y))

    fill_a = pltpu.make_async_copy(a_hbm, a_ref, fill_sem.at[0])
    fill_k = pltpu.make_async_copy(k_hbm, k_ref, fill_sem.at[1])
    fill_a.start()
    fill_k.start()

    barrier = pltpu.get_barrier_semaphore()
    partners = (
        [dict(dy=o) for o in range(1, Y)]
        + [dict(dzl=o) for o in range(1, ZL)]
        + [dict(dzh=o) for o in range(1, ZH)]
        + [dict(dx=1), dict(dx=-1), dict(dx=2), dict(dcore=1)]
    )
    for partner in partners:
        pl.semaphore_signal(barrier, inc=1, device_id=device(**partner), device_id_type=MESH)
    for s in range(S):
        for h in range(2):
            f_own[s, h] = f_ref[s, :, h * 128 : (h + 1) * 128]
            listed[s][y, h] = f_ref[s, :, h * 128 : (h + 1) * 128]
    pl.semaphore_wait(barrier, len(partners))

    ids, unsent = {}, []

    def copy(key, source, target, to):
        at = ids.setdefault(key, len(ids))
        return pltpu.make_async_remote_copy(
            src_ref=source, dst_ref=target, send_sem=send_sem.at[at], recv_sem=recv_sem.at[at],
            device_id=to, device_id_type=MESH,
        )

    def send(key, source, target, **to):
        made = copy(key, source, target, device(**to))
        made.start()
        unsent.append(made)

    def arrive(key, landed, **to):
        copy(key, landed, landed, device(**to)).wait_recv()

    lane_block = lax.broadcasted_iota(jnp.int32, (WP, 128), 1) // RB

    def gather_y(s):
        for o in (4, 3, 5, 2, 6, 1, 7):
            send(("y", s, o), f_own.at[s], listed[s].at[y], dy=o)

    def pick(s):
        for o in range(1, Y):
            arrive(("y", s, o), listed[s].at[turn(y, -o, Y)], dy=o)
        for part in range(ZL):
            for quad in range(NBC // QUAD):
                value = jnp.zeros((WP, 128), F32)
                for q in range(QUAD):
                    at = (s * TARGETS + part * NBC + quad * QUAD + q) * 3
                    source, shift, place = table[at], table[at + 1], table[at + 2]
                    block = pltpu.roll(listed[s][source // 2, lax.rem(source, 2)], shift, 1)
                    value = jnp.where(lane_block == place, block, value)
                picked[s, part, :, quad * 128 : (quad + 1) * 128] = value
        for o in (1, 2):
            send(("l", s, o), picked.at[s, turn(zl, o, ZL)], from_zl.at[s, o - 1], dzl=o)

    def own(s):
        for o in (1, 2):
            arrive(("l", s, o), from_zl.at[s, o - 1], dzl=o)
        factor[s, zh, x, core] = picked[s, zl] + (from_zl[s, 0] + from_zl[s, 1])
        piece = factor.at[s, zh, x, core]
        for o in (2, 1, 3):
            send(("h", s, o), piece, piece, dzh=o)
        along_x(s, 0)

    def along_x(s, o):
        piece = factor.at[s, turn(zh, -o, ZH), x, core]
        for by in (2, 1, -1):
            send(("x", s, o, by), piece, piece, dx=by)

    def from_zh(s, o):
        arrive(("h", s, o), factor.at[s, turn(zh, -o, ZH), x, core], dzh=o)
        along_x(s, o)

    def to_core(s, by):
        for o in range(ZH) if by else ():
            arrive(("x", s, o, by), factor.at[s, turn(zh, -o, ZH), turn(x, -by, X), core], dx=by)
        piece = factor.at[s, :, turn(x, -by, X), core]
        send(("c", s, by), piece, piece, dcore=1)

    def multiply(s):
        for by in (0, 1, -1, 2):
            arrive(("c", s, by), factor.at[s, :, turn(x, -by, X), 1 - core], dcore=1)
        b_high, b_low = split(factor[s].reshape(W, DEPTH))
        product = dot3(a_high[...], a_low[...], b_high, b_low, ((1,), (1,)))
        partial[s] = product.reshape(ZL, Y, OUT, W)
        if s in Z_FIRST:
            for group in range(5):
                for by in GROUPS[group]:
                    for o in (1, 2):
                        source = partial.at[s, turn(zl, o, ZL), turn(y, by, Y)]
                        send(("z", s, by, o), source, whole_in.at[Z_FIRST.index(s), o - 1, turn(y, by, Y)], dzl=o)
        else:
            for part in range(ZL):
                start_y(s, part)

    def start_y(s, part):
        for at, way, rows in ((0, 1, slice(0, 8)), (1, -1, slice(8, 16))):
            source = partial.at[s, turn(zl, part + 1, ZL), turn(y, 4, Y), rows]
            send(("r", s, part, 0, way), source, half_in.at[s, part, at], dy=way)

    def reduce_z(s, group):
        for by in GROUPS[group]:
            d = turn(y, by, Y)
            for o in (1, 2):
                arrive(("z", s, by, o), whole_in.at[Z_FIRST.index(s), o - 1, d], dzl=o)
            partial[s, zl, d] += whole_in[Z_FIRST.index(s), 0, d] + whole_in[Z_FIRST.index(s), 1, d]
        if group == 0:
            start_y(s, ZL - 1)

    def reduce_y(s, part, step):
        to = turn(zl, part + 1, ZL)
        for at, way, rows in ((0, 1, slice(0, 8)), (1, -1, slice(8, 16))):
            if step == 0:
                arrive(("r", s, part, 0, way), half_in.at[s, part, at], dy=way)
                partial[s, to, turn(y, 3 * way, Y), rows] += half_in[s, part, at]
            else:
                arrive(("r", s, part, step, way), step_in.at[s, part, at, step - 1], dy=way)
                partial[s, to, turn(y, (3 - step) * way, Y)] += step_in[s, part, at, step - 1]
            if step < 3:
                source = partial.at[s, to, turn(y, (3 - step) * way, Y)]
                send(("r", s, part, step + 1, way), source, step_in.at[s, part, at, step], dy=way)
        if step == 3 and part < ZL - 1:
            send(("w", s, part + 1), partial.at[s, to, y], last_in.at[s, part], dzl=part + 1)

    def finish(s):
        total = partial[s, zl, y]
        if s not in Z_FIRST:
            for o in (1, 2):
                arrive(("w", s, o), last_in.at[s, o - 1], dzl=o)
            total = total + (last_in[s, 0] + last_in[s, 1])
        if s:
            total = total + o_ref[s]
        total = -total
        o_ref[s] = total
        if s + 1 < S:
            high, low = split(total)
            o_ref[s + 1] = dot3(high, low, k_high[s], k_low[s], ((1,), (0,)))

    def prepare():
        fill_a.wait()
        fill_k.wait()
        a_high[...], a_low[...] = split(a_ref[...])
        k_high[...], k_low[...] = split(k_ref[...])

    events = (
        prepare, gather_y, pick, own, from_zh, to_core, multiply, reduce_z, reduce_y, finish,
    )
    for what, *given in ORDER:
        events[what](*given)
    for made in unsent:
        made.wait_send()


def fused(table, inverse_tiles, factor_panels, couplings):
    vmem = pl.BlockSpec(memory_space=pltpu.VMEM)
    anywhere = pl.BlockSpec(memory_space=pl.ANY)
    return pl.pallas_call(
        kernel,
        out_shape=jax.ShapeDtypeStruct((S, OUT, W), F32),
        in_specs=[pl.BlockSpec(memory_space=pltpu.SMEM), anywhere, vmem, anywhere],
        out_specs=vmem,
        scratch_shapes=[
            pltpu.VMEM((ROWS, DEPTH), F32),
            pltpu.VMEM((S - 1, W, W), F32),
            pltpu.VMEM((S, 2, WP, 128), F32),
            pltpu.VMEM((Y, 2, WP, 128), F32),
            pltpu.VMEM((Y, 2, WP, 128), F32),
            pltpu.VMEM((Y, 2, WP, 128), F32),
            pltpu.VMEM((S, ZL, WP, DEPTH), F32),
            pltpu.VMEM((S, 2, WP, DEPTH), F32),
            pltpu.VMEM((S, ZH, X, CORE, WP, DEPTH), F32),
            pltpu.VMEM((S, ZL, Y, OUT, W), F32),
            pltpu.VMEM((S, ZL, 2, OUT // 2, W), F32),
            pltpu.VMEM((S, ZL, 2, 3, OUT, W), F32),
            pltpu.VMEM((max(1, len(Z_FIRST)), 2, Y, OUT, W), F32),
            pltpu.VMEM((S, 2, OUT, W), F32),
            pltpu.VMEM((ROWS, DEPTH), BF16),
            pltpu.VMEM((ROWS, DEPTH), BF16),
            pltpu.VMEM((S - 1, W, W), BF16),
            pltpu.VMEM((S - 1, W, W), BF16),
            pltpu.SemaphoreType.DMA((2,)),
            pltpu.SemaphoreType.DMA((COPIES,)),
            pltpu.SemaphoreType.DMA((COPIES,)),
        ],
        compiler_params=pltpu.CompilerParams(
            collective_id=0, has_side_effects=True, vmem_limit_bytes=60 * 1024 * 1024
        ),
    )(table, inverse_tiles, factor_panels, couplings)


def on_device(inverse_tiles, factor_panels, block_rows, couplings):
    col = lax.axis_index("col")
    zl, y = col // Y, lax.rem(col, Y)
    target = jnp.arange(TARGETS, dtype=jnp.int32)
    wanted = (target // NBC * Y + y) * NBC + target % NBC
    number = jnp.arange(1, NZB + 1, dtype=jnp.int32)
    found = jnp.sum(
        jnp.where(block_rows[:, :, None] == wanted, number[:, None], 0), axis=1
    )
    local = found - 1 - zl * (Y * LISTED)
    here = (found > 0) & (local >= 0) & (local < Y * LISTED)
    local = jnp.where(here, local, 0)
    shift = jnp.where(here, (target - local) % QUAD * RB, 0)
    place = jnp.where(here, target % QUAD, QUAD)
    table = jnp.stack([local // QUAD, shift, place], axis=-1).reshape(-1)
    return fused(table, inverse_tiles, factor_panels, couplings)


def solution(mesh):
    return jax.shard_map(
        on_device,
        mesh=mesh,
        in_specs=(P("row", "col"), P(None, "row", "col"), P(), P()),
        out_specs=P(None, ("row", "col"), None),
        check_vma=False,
    )
```

```python
import jax
import jax.numpy as jnp
from jax import lax
from jax.experimental import pallas as pl
from jax.experimental.pallas import tpu as pltpu
from jax.sharding import PartitionSpec as P

ZH, X, CORE, ZL, Y = 4, 4, 2, 3, 8
S, W, RB, NBC, NZB = 3, 512, 32, 16, 192
WP = W // (ZH * X * CORE)
LISTED = NZB // (ZL * Y)
ROWS, DEPTH = 384, 512
OUT = ROWS // (ZL * Y)
TARGETS = ZL * NBC
WZ = W // ZH
QUAD = 128 // RB
MESH = pl.DeviceIdType.MESH
F32, BF16 = jnp.float32, jnp.bfloat16
SENDS, ARRIVALS = 9, 78
PARTS = ((0,), (1, 3), (2,))
STEPS = tuple(o for part in PARTS for o in part)
HOP_ORDER = ((1, 3, 2), (1, 3, 2), (1, 3, 2))
ORDER = (
    (1, 0), (1, 1), (0,), (1, 2), (2, 0), (2, 1), (3, 0), (2, 2), (3, 1), (5, 0, 0), (6, 0, 0), (4, 0, 1),
    (4, 0, 3), (5, 1, 0), (6, 1, 0), (7, 0, 0, 0), (3, 2), (4, 0, 2), (4, 1, 1), (4, 1, 3), (5, 0, 1),
    (7, 1, 0, 0), (7, 0, 0, 1), (5, 2, 0), (6, 0, 1), (5, 0, 2), (6, 2, 0), (7, 1, 0, 1), (4, 1, 2),
    (4, 2, 1), (7, 0, 0, 2), (4, 2, 3), (6, 0, 2), (7, 0, 1, 0), (5, 1, 1), (7, 2, 0, 0), (7, 1, 0, 2),
    (7, 0, 0, 3), (4, 2, 2), (7, 0, 2, 0), (6, 1, 1), (5, 1, 2), (7, 0, 1, 1), (7, 2, 0, 1), (6, 1, 2),
    (8, 0, 0), (7, 0, 2, 1), (7, 1, 0, 3), (5, 2, 1), (7, 1, 1, 0), (5, 2, 2), (7, 0, 1, 2), (6, 2, 1),
    (6, 2, 2), (7, 1, 2, 0), (7, 0, 2, 2), (7, 2, 0, 2), (7, 1, 1, 1), (7, 0, 1, 3), (7, 2, 1, 0),
    (7, 2, 2, 0), (7, 1, 2, 1), (7, 0, 2, 3), (7, 2, 0, 3), (7, 1, 1, 2), (8, 0, 1), (7, 2, 1, 1),
    (7, 2, 2, 1), (8, 0, 2), (9, 0), (8, 1, 0), (7, 1, 2, 2), (7, 1, 1, 3), (7, 2, 1, 2), (7, 2, 2, 2),
    (7, 1, 2, 3), (8, 1, 1), (7, 2, 1, 3), (7, 2, 2, 3), (8, 1, 2), (9, 1), (8, 2, 0), (8, 2, 1), (8, 2, 2),
)


def split(value):
    high = value.astype(BF16)
    return high, (value - high.astype(F32)).astype(BF16)


def dot3(a_high, a_low, b_high, b_low, dims):
    def one(a, b):
        return lax.dot_general(a, b, (dims, ((), ())), preferred_element_type=F32)

    return one(a_high, b_high) + (one(a_high, b_low) + one(a_low, b_high))


def kernel(
    table, a_hbm, f_hbm, k_hbm, o_ref,
    a_ref, k_ref, f_own, listed_0, listed_1, listed_2, picked, from_zl, factor, partial,
    half_in, step_in, last_in, a_high, a_low, k_high, k_low, fill_sem, send_sem, recv_sem,
):
    row, col = lax.axis_index("row"), lax.axis_index("col")
    zh, x, core = row // (X * CORE), lax.rem(row // CORE, X), lax.rem(row, CORE)
    zl, y = col // Y, lax.rem(col, Y)
    listed = (listed_0, listed_1, listed_2)

    def turn(value, by, size):
        return lax.rem(value + (by + size), size)

    def device(dzh=0, dx=0, dcore=0, dzl=0, dy=0):
        at_row = (turn(zh, dzh, ZH) * X + turn(x, dx, X)) * CORE + (1 - core if dcore else core)
        return (at_row, turn(zl, dzl, ZL) * Y + turn(y, dy, Y))

    fill_f = [
        pltpu.make_async_copy(f_hbm.at[:, :, pl.ds(h * 128, 128)], f_own.at[:, h], fill_sem.at[h])
        for h in range(2)
    ]
    fill_a = pltpu.make_async_copy(a_hbm, a_ref, fill_sem.at[2])
    fill_k = pltpu.make_async_copy(k_hbm, k_ref, fill_sem.at[3])
    for fill in (*fill_f, fill_a, fill_k):
        fill.start()

    barrier = pltpu.get_barrier_semaphore()
    partners = (
        [dict(dy=o) for o in range(1, Y)]
        + [dict(dzl=o) for o in range(1, ZL)]
        + [dict(dzh=o) for o in range(1, ZH)]
        + [dict(dx=1), dict(dx=-1), dict(dx=2), dict(dcore=1)]
    )
    for partner in partners:
        pl.semaphore_signal(barrier, inc=1, device_id=device(**partner), device_id_type=MESH)
    for fill in fill_f:
        fill.wait()
    pl.semaphore_wait(barrier, len(partners))

    arrivals, sends = {}, {}

    def copy(sent, key, source, target, to):
        out, into = sends.setdefault(sent, len(sends)), arrivals.setdefault(key, len(arrivals))
        return pltpu.make_async_remote_copy(
            src_ref=source, dst_ref=target, send_sem=send_sem.at[out], recv_sem=recv_sem.at[into],
            device_id=to, device_id_type=MESH,
        )

    def send(sent, key, source, target, **to):
        copy(sent, key, source, target, device(**to)).start()

    def arrive(key, landed):
        copy(("y", 0), key, landed, landed, device(dcore=1)).wait_recv()

    def all_sent(sent, as_large):
        copy(sent, ("y", 0), as_large, as_large, device(dcore=1)).wait_send()

    lane_block = lax.broadcasted_iota(jnp.int32, (WP, 128), 1) // RB

    def gather_y(s):
        for o in (4, 3, 5, 2, 6, 1, 7):
            send(("y", s), ("y", s), f_own.at[s], listed[s].at[o - 1], dy=o)
        for h in range(2):
            listed[s][Y - 1, h] = f_own[s, h]

    def pick(s):
        arrive(("y", s), listed[s].at[0 : Y - 1])
        for part in range(ZL):
            for quad in range(NBC // QUAD):
                value = jnp.zeros((WP, 128), F32)
                for q in range(QUAD):
                    code = table[s, part * NBC + quad * QUAD + q]
                    tile = lax.min(code // QUAD, 2 * Y - 1)
                    shift = lax.rem(q + QUAD - lax.rem(code, QUAD), QUAD) * RB
                    place = jnp.where(code < Y * LISTED, q, QUAD)
                    block = pltpu.roll(listed[s][tile // 2, lax.rem(tile, 2)], shift, 1)
                    value = jnp.where(lane_block == place, block, value)
                picked[s, part, :, quad * 128 : (quad + 1) * 128] = value
        for o in (1, 2):
            send("l", ("l", s), picked.at[s, turn(zl, o, ZL)], from_zl.at[s, o - 1], dzl=o)

    def slots(part):
        first = STEPS.index(PARTS[part][0])
        return slice(first, first + len(PARTS[part]))

    def own(s):
        arrive(("l", s), from_zl.at[s])
        factor[s, 0, x, core] = picked[s, zl] + (from_zl[s, 0] + from_zl[s, 1])
        for o in HOP_ORDER[s]:
            send("h", ("h", s, o), factor.at[s, 0, x, core], factor.at[s, STEPS.index(o), x, core], dzh=o)
        along_x(s, 0)

    def along_x(s, o):
        piece = factor.at[s, STEPS.index(o), x, core]
        part = [o in steps for steps in PARTS].index(True)
        for by in (2, 1, -1):
            send("x", ("x", s, part), piece, piece, dx=by)

    def from_zh(s, o):
        arrive(("h", s, o), factor.at[s, STEPS.index(o), x, core])
        along_x(s, o)

    def to_core(s, part):
        arrive(("x", s, part), factor.at[s, slots(part), 0 : X - 1, core])
        pieces = factor.at[s, slots(part), :, core]
        send("c", ("c", s, part), pieces, pieces, dcore=1)

    def multiply(s, part):
        arrive(("c", s, part), factor.at[s, slots(part), :, 1 - core])
        count = len(PARTS[part])
        b_high, b_low = split(factor[s, slots(part)].reshape(count * WZ, DEPTH))
        product = dot3(a_high[...], a_low[...], b_high, b_low, ((1,), (1,)))
        for n in range(count):
            columns = product[:, n * WZ : (n + 1) * WZ]
            partial[s, slots(part).start + n] = columns.reshape(ZL, Y, OUT, WZ)
        for at, way, rows in ((0, 1, slice(0, 8)), (1, -1, slice(8, 16))):
            source = partial.at[s, slots(part), :, turn(y, 4, Y), rows]
            send("r", ("r", s, part, 0), source, half_in.at[s, at, slots(part)], dy=way)

    def reduce_y(s, part, step):
        at_part = slots(part)
        if step == 0:
            arrive(("r", s, part, 0), half_in.at[s, :, at_part])
        else:
            arrive(("r", s, part, step), step_in.at[s, step - 1, :, at_part])
        for at, way, rows in ((0, 1, slice(0, 8)), (1, -1, slice(8, 16))):
            if step == 0:
                partial[s, at_part, :, turn(y, 3 * way, Y), rows] += half_in[s, at, at_part]
            else:
                partial[s, at_part, :, turn(y, (3 - step) * way, Y)] += step_in[s, step - 1, at, at_part]
            if step < 3:
                source = partial.at[s, at_part, :, turn(y, (3 - step) * way, Y)]
                send("r", ("r", s, part, step + 1), source, step_in.at[s, step, at, at_part], dy=way)
        if step == 3:
            for o in (1, 2):
                source = partial.at[s, at_part, turn(zl, o, ZL), y]
                send("w", ("w", s, part), source, last_in.at[s, o - 1, at_part], dzl=o)

    def finish(s, part):
        arrive(("w", s, part), last_in.at[s, :, slots(part)])
        for o in PARTS[part]:
            at = STEPS.index(o)
            columns = pl.ds(pl.multiple_of(turn(zh, -o, ZH) * WZ, WZ), WZ)
            total = partial[s, at, zl, y] + (last_in[s, 0, at] + last_in[s, 1, at])
            if s:
                total = total + o_ref[s, :, columns]
            o_ref[s, :, columns] = -total

    def couple(s):
        high, low = split(o_ref[s])
        o_ref[s + 1] = dot3(high, low, k_high[s], k_low[s], ((1,), (0,)))

    def prepare():
        fill_a.wait()
        fill_k.wait()
        a_high[...], a_low[...] = split(a_ref[...])
        k_high[...], k_low[...] = split(k_ref[...])

    events = (
        prepare, gather_y, pick, own, from_zh, to_core, multiply, reduce_y, finish, couple,
    )
    for what, *given in ORDER:
        events[what](*given)
    all_sent("l", from_zl)
    all_sent("h", picked)
    all_sent("x", factor.at[:, :, 0:3, 0])
    all_sent("c", factor.at[:, :, :, 0])
    for s in range(S):
        all_sent(("y", s), listed[s].at[0 : Y - 1])
    all_sent("r", partial.at[:, :, :, 0 : Y - 1])
    all_sent("w", last_in)
    assert (len(sends), len(arrivals)) == (SENDS, ARRIVALS)


def fused(table, inverse_tiles, factor_panels, couplings):
    hbm = pl.BlockSpec(memory_space=pltpu.HBM)
    return pl.pallas_call(
        kernel,
        out_shape=jax.ShapeDtypeStruct((S, OUT, W), F32),
        in_specs=[pl.BlockSpec(memory_space=pltpu.SMEM), hbm, hbm, hbm],
        out_specs=pl.BlockSpec(memory_space=pltpu.VMEM),
        scratch_shapes=[
            pltpu.VMEM((ROWS, DEPTH), F32),
            pltpu.VMEM((S - 1, W, W), F32),
            pltpu.VMEM((S, 2, WP, 128), F32),
            pltpu.VMEM((Y, 2, WP, 128), F32),
            pltpu.VMEM((Y, 2, WP, 128), F32),
            pltpu.VMEM((Y, 2, WP, 128), F32),
            pltpu.VMEM((S, ZL, WP, DEPTH), F32),
            pltpu.VMEM((S, 2, WP, DEPTH), F32),
            pltpu.VMEM((S, ZH, X, CORE, WP, DEPTH), F32),
            pltpu.VMEM((S, ZH, ZL, Y, OUT, WZ), F32),
            pltpu.VMEM((S, 2, ZH, ZL, OUT // 2, WZ), F32),
            pltpu.VMEM((S, 3, 2, ZH, ZL, OUT, WZ), F32),
            pltpu.VMEM((S, 2, ZH, OUT, WZ), F32),
            pltpu.VMEM((ROWS, DEPTH), BF16),
            pltpu.VMEM((ROWS, DEPTH), BF16),
            pltpu.VMEM((S - 1, W, W), BF16),
            pltpu.VMEM((S - 1, W, W), BF16),
            pltpu.SemaphoreType.DMA((4,)),
            pltpu.SemaphoreType.DMA((SENDS,)),
            pltpu.SemaphoreType.DMA((ARRIVALS,)),
        ],
        compiler_params=pltpu.CompilerParams(
            collective_id=0, has_side_effects=True, vmem_limit_bytes=60 * 1024 * 1024
        ),
    )(table, inverse_tiles, factor_panels, couplings)


def on_device(inverse_tiles, factor_panels, block_rows, couplings):
    col = lax.axis_index("col")
    zl, y = col // Y, lax.rem(col, Y)
    target = jnp.arange(TARGETS, dtype=jnp.int32)
    wanted = (target // NBC * Y + y) * NBC + target % NBC
    number = jnp.arange(1, NZB + 1, dtype=jnp.int32)
    found = jnp.sum(
        jnp.where(block_rows[:, :, None] == wanted, number[:, None], 0), axis=1
    )
    local = found - 1 - zl * (Y * LISTED)
    here = (found > 0) & (local >= 0) & (local < Y * LISTED)
    slot = (y + (Y - 1) - local // LISTED) % Y
    code = jnp.where(here, slot * LISTED + local % LISTED, Y * LISTED)
    return fused(code, inverse_tiles, factor_panels, couplings)


def solution(mesh):
    return jax.shard_map(
        on_device,
        mesh=mesh,
        in_specs=(P("row", "col"), P(None, "row", "col"), P(), P()),
        out_specs=P(None, ("row", "col"), None),
        check_vma=False,
    )
```

```python
import jax
import jax.numpy as jnp
from jax import lax
from jax.experimental import pallas as pl
from jax.experimental.pallas import tpu as pltpu
from jax.sharding import PartitionSpec as P

ZH, X, CORE, ZL, Y = 4, 4, 2, 3, 8
S, W, RB, NBC, NZB = 3, 512, 32, 16, 192
WP = W // (ZH * X * CORE)
LISTED = NZB // (ZL * Y)
ROWS, DEPTH = 384, 512
OUT = ROWS // (ZL * Y)
TARGETS = ZL * NBC
WZ = W // ZH
QUAD = 128 // RB
MESH = pl.DeviceIdType.MESH
F32, BF16 = jnp.float32, jnp.bfloat16
SENDS, ARRIVALS = 9, 78
PARTS = ((0,), (1, 3), (2,))
STEPS = tuple(o for part in PARTS for o in part)
RELAYED = (0, 1, 2)
ORDER = (
    (1, 0), (1, 2), (0,), (1, 1), (2, 0), (2, 2), (3, 0), (2, 1), (3, 2), (5, 0, 0), (6, 0, 0), (4, 0, 3),
    (4, 0, 1), (5, 2, 0), (3, 1), (6, 2, 0), (7, 0, 0, 0), (4, 2, 1), (4, 2, 3), (4, 0, 2), (5, 0, 1),
    (7, 2, 0, 0), (7, 0, 0, 1), (5, 1, 0), (4, 1, 3), (4, 1, 1), (6, 0, 1), (4, 2, 2), (6, 1, 0),
    (7, 0, 0, 2), (5, 2, 1), (7, 2, 0, 1), (5, 0, 2), (7, 0, 1, 0), (4, 1, 2), (6, 2, 1), (6, 0, 2),
    (7, 2, 0, 2), (7, 0, 0, 3), (7, 1, 0, 0), (5, 1, 1), (7, 0, 1, 1), (5, 2, 2), (5, 1, 2), (7, 2, 1, 0),
    (7, 0, 2, 0), (6, 1, 1), (6, 1, 2), (7, 1, 0, 1), (7, 0, 1, 2), (8, 0, 0), (6, 2, 2), (7, 0, 2, 1),
    (7, 1, 1, 0), (7, 2, 1, 1), (7, 1, 2, 0), (7, 2, 0, 3), (7, 1, 0, 2), (7, 0, 1, 3), (7, 2, 2, 0),
    (7, 0, 2, 2), (7, 1, 1, 1), (7, 2, 1, 2), (7, 1, 2, 1), (8, 0, 1), (7, 1, 0, 3), (7, 2, 2, 1),
    (7, 0, 2, 3), (7, 1, 1, 2), (7, 2, 1, 3), (7, 1, 2, 2), (7, 2, 2, 2), (8, 0, 2), (9, 0), (8, 1, 0),
    (7, 1, 1, 3), (7, 1, 2, 3), (7, 2, 2, 3), (8, 1, 1), (8, 1, 2), (9, 1), (8, 2, 1), (8, 2, 2), (8, 2, 0),
)


def split(value):
    high = value.astype(BF16)
    return high, (value - high.astype(F32)).astype(BF16)


def dot3(a_high, a_low, b_high, b_low, dims):
    def one(a, b):
        return lax.dot_general(a, b, (dims, ((), ())), preferred_element_type=F32)

    return one(a_high, b_high) + (one(a_high, b_low) + one(a_low, b_high))


def kernel(
    table, a_hbm, f_hbm, k_hbm, o_ref,
    a_ref, k_ref, f_own, listed_0, listed_1, listed_2, picked, from_zl, factor, partial,
    half_in, step_in, last_in, a_high, a_low, k_high, k_low, fill_sem, send_sem, recv_sem,
):
    row, col = lax.axis_index("row"), lax.axis_index("col")
    zh, x, core = row // (X * CORE), lax.rem(row // CORE, X), lax.rem(row, CORE)
    zl, y = col // Y, lax.rem(col, Y)
    listed = (listed_0, listed_1, listed_2)

    def turn(value, by, size):
        return lax.rem(value + (by + size), size)

    def device(dzh=0, dx=0, dcore=0, dzl=0, dy=0):
        at_row = (turn(zh, dzh, ZH) * X + turn(x, dx, X)) * CORE + (1 - core if dcore else core)
        return (at_row, turn(zl, dzl, ZL) * Y + turn(y, dy, Y))

    fill_f = [
        pltpu.make_async_copy(f_hbm.at[:, :, pl.ds(h * 128, 128)], f_own.at[:, h], fill_sem.at[h])
        for h in range(2)
    ]
    fill_a = pltpu.make_async_copy(a_hbm, a_ref, fill_sem.at[2])
    fill_k = pltpu.make_async_copy(k_hbm, k_ref, fill_sem.at[3])
    for fill in (*fill_f, fill_a, fill_k):
        fill.start()

    barrier = pltpu.get_barrier_semaphore()
    partners = (
        [dict(dy=o) for o in range(1, Y)]
        + [dict(dzl=o) for o in range(1, ZL)]
        + [dict(dzh=o) for o in range(1, ZH)]
        + [dict(dx=1), dict(dx=-1), dict(dx=2), dict(dcore=1)]
    )
    for partner in partners:
        pl.semaphore_signal(barrier, inc=1, device_id=device(**partner), device_id_type=MESH)
    for fill in fill_f:
        fill.wait()
    pl.semaphore_wait(barrier, len(partners))

    arrivals, sends = {}, {}

    def copy(sent, key, source, target, to):
        out, into = sends.setdefault(sent, len(sends)), arrivals.setdefault(key, len(arrivals))
        return pltpu.make_async_remote_copy(
            src_ref=source, dst_ref=target, send_sem=send_sem.at[out], recv_sem=recv_sem.at[into],
            device_id=to, device_id_type=MESH,
        )

    def send(sent, key, source, target, **to):
        copy(sent, key, source, target, device(**to)).start()

    def arrive(key, landed):
        copy(("y", 0), key, landed, landed, device(dcore=1)).wait_recv()

    def all_sent(sent, as_large):
        copy(sent, ("y", 0), as_large, as_large, device(dcore=1)).wait_send()

    lane_block = lax.broadcasted_iota(jnp.int32, (WP, 128), 1) // RB

    def gather_y(s):
        for o in (4, 3, 5, 2, 6, 1, 7):
            send(("y", s), ("y", s), f_own.at[s], listed[s].at[o - 1], dy=o)
        for h in range(2):
            listed[s][Y - 1, h] = f_own[s, h]

    def pick(s):
        arrive(("y", s), listed[s].at[0 : Y - 1])
        for part in range(ZL):
            for quad in range(NBC // QUAD):
                value = jnp.zeros((WP, 128), F32)
                for q in range(QUAD):
                    code = table[s, part * NBC + quad * QUAD + q]
                    tile = lax.min(code // QUAD, 2 * Y - 1)
                    shift = lax.rem(q + QUAD - lax.rem(code, QUAD), QUAD) * RB
                    place = jnp.where(code < Y * LISTED, q, QUAD)
                    block = pltpu.roll(listed[s][tile // 2, lax.rem(tile, 2)], shift, 1)
                    value = jnp.where(lane_block == place, block, value)
                picked[s, part, :, quad * 128 : (quad + 1) * 128] = value
        for o in (1, 2):
            send("l", ("l", s), picked.at[s, turn(zl, o, ZL)], from_zl.at[s, o - 1], dzl=o)

    def slots(part):
        first = STEPS.index(PARTS[part][0])
        return slice(first, first + len(PARTS[part]))

    def own(s):
        arrive(("l", s), from_zl.at[s])
        factor[s, 0, x, core] = picked[s, zl] + (from_zl[s, 0] + from_zl[s, 1])
        for o in (1, 3) if s in RELAYED else (1, 3, 2):
            send("h", ("h", s, o), factor.at[s, 0, x, core], factor.at[s, STEPS.index(o), x, core], dzh=o)
        along_x(s, 0)

    def along_x(s, o):
        piece = factor.at[s, STEPS.index(o), x, core]
        part = [o in steps for steps in PARTS].index(True)
        for by in (2, 1, -1):
            send("x", ("x", s, part), piece, piece, dx=by)

    def from_zh(s, o):
        arrive(("h", s, o), factor.at[s, STEPS.index(o), x, core])
        if s in RELAYED and o != 2:
            half = slice(0, WP // 2) if o == 1 else slice(WP // 2, WP)
            source = factor.at[s, STEPS.index(o), x, core, half]
            send("h", ("h", s, 2), source, factor.at[s, STEPS.index(2), x, core, half], dzh=o)
        along_x(s, o)

    def to_core(s, part):
        arrive(("x", s, part), factor.at[s, slots(part), 0 : X - 1, core])
        pieces = factor.at[s, slots(part), :, core]
        send("c", ("c", s, part), pieces, pieces, dcore=1)

    def multiply(s, part):
        arrive(("c", s, part), factor.at[s, slots(part), :, 1 - core])
        count = len(PARTS[part])
        b_high, b_low = split(factor[s, slots(part)].reshape(count * WZ, DEPTH))
        product = dot3(a_high[...], a_low[...], b_high, b_low, ((1,), (1,)))
        for n in range(count):
            columns = product[:, n * WZ : (n + 1) * WZ]
            partial[s, slots(part).start + n] = columns.reshape(ZL, Y, OUT, WZ)
        for at, way, rows in ((0, 1, slice(0, 8)), (1, -1, slice(8, 16))):
            source = partial.at[s, slots(part), :, turn(y, 4, Y), rows]
            send("r", ("r", s, part, 0), source, half_in.at[s, at, slots(part)], dy=way)

    def reduce_y(s, part, step):
        at_part = slots(part)
        if step == 0:
            arrive(("r", s, part, 0), half_in.at[s, :, at_part])
        else:
            arrive(("r", s, part, step), step_in.at[s, step - 1, :, at_part])
        for at, way, rows in ((0, 1, slice(0, 8)), (1, -1, slice(8, 16))):
            if step == 0:
                partial[s, at_part, :, turn(y, 3 * way, Y), rows] += half_in[s, at, at_part]
            else:
                partial[s, at_part, :, turn(y, (3 - step) * way, Y)] += step_in[s, step - 1, at, at_part]
            if step < 3:
                source = partial.at[s, at_part, :, turn(y, (3 - step) * way, Y)]
                send("r", ("r", s, part, step + 1), source, step_in.at[s, step, at, at_part], dy=way)
        if step == 3:
            for o in (1, 2):
                source = partial.at[s, at_part, turn(zl, o, ZL), y]
                send("w", ("w", s, part), source, last_in.at[s, o - 1, at_part], dzl=o)

    def finish(s, part):
        arrive(("w", s, part), last_in.at[s, :, slots(part)])
        for o in PARTS[part]:
            at = STEPS.index(o)
            columns = pl.ds(pl.multiple_of(turn(zh, -o, ZH) * WZ, WZ), WZ)
            total = partial[s, at, zl, y] + (last_in[s, 0, at] + last_in[s, 1, at])
            if s:
                total = total + o_ref[s, :, columns]
            o_ref[s, :, columns] = -total

    def couple(s):
        high, low = split(o_ref[s])
        o_ref[s + 1] = dot3(high, low, k_high[s], k_low[s], ((1,), (0,)))

    def prepare():
        fill_a.wait()
        fill_k.wait()
        a_high[...], a_low[...] = split(a_ref[...])
        k_high[...], k_low[...] = split(k_ref[...])

    events = (
        prepare, gather_y, pick, own, from_zh, to_core, multiply, reduce_y, finish, couple,
    )
    for what, *given in ORDER:
        events[what](*given)
    all_sent("l", from_zl)
    all_sent("h", picked)
    all_sent("x", factor.at[:, :, 0:3, 0])
    all_sent("c", factor.at[:, :, :, 0])
    for s in range(S):
        all_sent(("y", s), listed[s].at[0 : Y - 1])
    all_sent("r", partial.at[:, :, :, 0 : Y - 1])
    all_sent("w", last_in)
    assert (len(sends), len(arrivals)) == (SENDS, ARRIVALS)


def fused(table, inverse_tiles, factor_panels, couplings):
    hbm = pl.BlockSpec(memory_space=pltpu.HBM)
    return pl.pallas_call(
        kernel,
        out_shape=jax.ShapeDtypeStruct((S, OUT, W), F32),
        in_specs=[pl.BlockSpec(memory_space=pltpu.SMEM), hbm, hbm, hbm],
        out_specs=pl.BlockSpec(memory_space=pltpu.VMEM),
        scratch_shapes=[
            pltpu.VMEM((ROWS, DEPTH), F32),
            pltpu.VMEM((S - 1, W, W), F32),
            pltpu.VMEM((S, 2, WP, 128), F32),
            pltpu.VMEM((Y, 2, WP, 128), F32),
            pltpu.VMEM((Y, 2, WP, 128), F32),
            pltpu.VMEM((Y, 2, WP, 128), F32),
            pltpu.VMEM((S, ZL, WP, DEPTH), F32),
            pltpu.VMEM((S, 2, WP, DEPTH), F32),
            pltpu.VMEM((S, ZH, X, CORE, WP, DEPTH), F32),
            pltpu.VMEM((S, ZH, ZL, Y, OUT, WZ), F32),
            pltpu.VMEM((S, 2, ZH, ZL, OUT // 2, WZ), F32),
            pltpu.VMEM((S, 3, 2, ZH, ZL, OUT, WZ), F32),
            pltpu.VMEM((S, 2, ZH, OUT, WZ), F32),
            pltpu.VMEM((ROWS, DEPTH), BF16),
            pltpu.VMEM((ROWS, DEPTH), BF16),
            pltpu.VMEM((S - 1, W, W), BF16),
            pltpu.VMEM((S - 1, W, W), BF16),
            pltpu.SemaphoreType.DMA((4,)),
            pltpu.SemaphoreType.DMA((SENDS,)),
            pltpu.SemaphoreType.DMA((ARRIVALS,)),
        ],
        compiler_params=pltpu.CompilerParams(
            collective_id=0, has_side_effects=True, vmem_limit_bytes=60 * 1024 * 1024
        ),
    )(table, inverse_tiles, factor_panels, couplings)


def on_device(inverse_tiles, factor_panels, block_rows, couplings):
    col = lax.axis_index("col")
    zl, y = col // Y, lax.rem(col, Y)
    target = jnp.arange(TARGETS, dtype=jnp.int32)
    wanted = (target // NBC * Y + y) * NBC + target % NBC
    number = jnp.arange(1, NZB + 1, dtype=jnp.int32)
    found = jnp.sum(
        jnp.where(block_rows[:, :, None] == wanted, number[:, None], 0), axis=1
    )
    local = found - 1 - zl * (Y * LISTED)
    here = (found > 0) & (local >= 0) & (local < Y * LISTED)
    slot = (y + (Y - 1) - local // LISTED) % Y
    code = jnp.where(here, slot * LISTED + local % LISTED, Y * LISTED)
    return fused(code, inverse_tiles, factor_panels, couplings)


def solution(mesh):
    return jax.shard_map(
        on_device,
        mesh=mesh,
        in_specs=(P("row", "col"), P(None, "row", "col"), P(), P()),
        out_specs=P(None, ("row", "col"), None),
        check_vma=False,
    )
```

```python
import jax
import jax.numpy as jnp
from jax import lax
from jax.experimental import pallas as pl
from jax.experimental.pallas import tpu as pltpu
from jax.sharding import PartitionSpec as P

ZH, X, CORE, ZL, Y = 4, 4, 2, 3, 8
S, W, RB, NBC, NZB = 3, 512, 32, 16, 192
WP = W // (ZH * X * CORE)
LISTED = NZB // (ZL * Y)
ROWS, DEPTH = 384, 512
OUT = ROWS // (ZL * Y)
TARGETS = ZL * NBC
WZ = W // ZH
QUAD = 128 // RB
MESH = pl.DeviceIdType.MESH
F32, BF16 = jnp.float32, jnp.bfloat16
SENDS, ARRIVALS = 9, 78
PARTS = ((0,), (1, 3), (2,))
STEPS = tuple(o for part in PARTS for o in part)
RELAYED = (0, 1, 2)
ORDER = (
    (1, 0), (1, 2), (0,), (1, 1), (2, 0), (2, 2), (3, 0), (2, 1), (3, 2), (5, 0, 0), (6, 0, 0), (4, 0, 3),
    (4, 0, 1), (5, 2, 0), (3, 1), (6, 2, 0), (7, 0, 0, 0), (4, 2, 1), (4, 2, 3), (4, 0, 2), (5, 0, 1),
    (7, 2, 0, 0), (7, 0, 0, 1), (5, 1, 0), (4, 1, 3), (4, 1, 1), (6, 0, 1), (4, 2, 2), (6, 1, 0),
    (7, 0, 0, 2), (5, 2, 1), (7, 2, 0, 1), (5, 0, 2), (7, 0, 1, 0), (4, 1, 2), (6, 2, 1), (6, 0, 2),
    (7, 2, 0, 2), (7, 0, 0, 3), (7, 1, 0, 0), (5, 1, 1), (7, 0, 1, 1), (5, 2, 2), (5, 1, 2), (7, 2, 1, 0),
    (7, 0, 2, 0), (6, 1, 1), (6, 1, 2), (7, 1, 0, 1), (7, 0, 1, 2), (8, 0, 0), (6, 2, 2), (7, 0, 2, 1),
    (7, 1, 1, 0), (7, 2, 1, 1), (7, 1, 2, 0), (7, 2, 0, 3), (7, 1, 0, 2), (7, 0, 1, 3), (7, 2, 2, 0),
    (7, 0, 2, 2), (7, 1, 1, 1), (7, 2, 1, 2), (7, 1, 2, 1), (8, 0, 1), (7, 1, 0, 3), (7, 2, 2, 1),
    (7, 0, 2, 3), (7, 1, 1, 2), (7, 2, 1, 3), (7, 1, 2, 2), (7, 2, 2, 2), (8, 0, 2), (9, 0), (8, 1, 0),
    (7, 1, 1, 3), (7, 1, 2, 3), (7, 2, 2, 3), (8, 1, 1), (8, 1, 2), (9, 1), (8, 2, 1), (8, 2, 2), (8, 2, 0),
)


def split(value):
    high = value.astype(BF16)
    return high, (value - high.astype(F32)).astype(BF16)


def dot3(a_high, a_low, b_high, b_low, dims):
    def one(a, b):
        return lax.dot_general(a, b, (dims, ((), ())), preferred_element_type=F32)

    return one(a_high, b_high) + (one(a_high, b_low) + one(a_low, b_high))


def kernel(
    table, a_hbm, f_hbm, k_hbm, o_ref,
    a_ref, k_ref, f_own, listed_0, listed_1, listed_2, picked, from_zl, factor, partial,
    half_in, step_in, last_in, a_high, a_low, k_high, k_low, fill_sem, send_sem, recv_sem,
):
    row, col = lax.axis_index("row"), lax.axis_index("col")
    zh, x, core = row // (X * CORE), lax.rem(row // CORE, X), lax.rem(row, CORE)
    zl, y = col // Y, lax.rem(col, Y)
    listed = (listed_0, listed_1, listed_2)

    def turn(value, by, size):
        return lax.rem(value + (by + size), size)

    def device(dzh=0, dx=0, dcore=0, dzl=0, dy=0):
        at_row = (turn(zh, dzh, ZH) * X + turn(x, dx, X)) * CORE + (1 - core if dcore else core)
        return (at_row, turn(zl, dzl, ZL) * Y + turn(y, dy, Y))

    fill_f = [
        pltpu.make_async_copy(f_hbm.at[:, :, pl.ds(h * 128, 128)], f_own.at[:, h], fill_sem.at[h])
        for h in range(2)
    ]
    fill_a = pltpu.make_async_copy(a_hbm, a_ref, fill_sem.at[2])
    fill_k = pltpu.make_async_copy(k_hbm, k_ref, fill_sem.at[3])
    for fill in (*fill_f, fill_a, fill_k):
        fill.start()

    barrier = pltpu.get_barrier_semaphore()
    partners = (
        [dict(dy=o) for o in range(1, Y)]
        + [dict(dzl=o) for o in range(1, ZL)]
        + [dict(dzh=o) for o in range(1, ZH)]
        + [dict(dx=1), dict(dx=-1), dict(dx=2), dict(dcore=1)]
    )
    for partner in partners:
        pl.semaphore_signal(barrier, inc=1, device_id=device(**partner), device_id_type=MESH)
    for fill in fill_f:
        fill.wait()
    pl.semaphore_wait(barrier, len(partners))

    arrivals, sends = {}, {}

    def copy(sent, key, source, target, to):
        out, into = sends.setdefault(sent, len(sends)), arrivals.setdefault(key, len(arrivals))
        return pltpu.make_async_remote_copy(
            src_ref=source, dst_ref=target, send_sem=send_sem.at[out], recv_sem=recv_sem.at[into],
            device_id=to, device_id_type=MESH,
        )

    def send(sent, key, source, target, **to):
        copy(sent, key, source, target, device(**to)).start()

    def arrive(key, landed):
        copy(("y", 0), key, landed, landed, device(dcore=1)).wait_recv()

    def all_sent(sent, as_large):
        copy(sent, ("y", 0), as_large, as_large, device(dcore=1)).wait_send()

    lane_block = lax.broadcasted_iota(jnp.int32, (WP, 128), 1) // RB

    def gather_y(s):
        for o in (4, 3, 5, 2, 6, 1, 7):
            send(("y", s), ("y", s), f_own.at[s], listed[s].at[o - 1], dy=o)
        for h in range(2):
            listed[s][Y - 1, h] = f_own[s, h]

    def pick(s):
        arrive(("y", s), listed[s].at[0 : Y - 1])
        for part in range(ZL):
            for quad in range(NBC // QUAD):
                value = jnp.zeros((WP, 128), F32)
                for q in range(QUAD):
                    code = table[s, part * NBC + quad * QUAD + q]
                    tile = lax.min(code // QUAD, 2 * Y - 1)
                    shift = lax.rem(q + QUAD - lax.rem(code, QUAD), QUAD) * RB
                    place = jnp.where(code < Y * LISTED, q, QUAD)
                    block = pltpu.roll(listed[s][tile // 2, lax.rem(tile, 2)], shift, 1)
                    value = jnp.where(lane_block == place, block, value)
                picked[s, part, :, quad * 128 : (quad + 1) * 128] = value
        for o in (1, 2):
            send("l", ("l", s), picked.at[s, turn(zl, o, ZL)], from_zl.at[s, o - 1], dzl=o)

    def slots(part):
        first = STEPS.index(PARTS[part][0])
        return slice(first, first + len(PARTS[part]))

    def own(s):
        arrive(("l", s), from_zl.at[s])
        factor[s, 0, x, core] = picked[s, zl] + (from_zl[s, 0] + from_zl[s, 1])
        for o in (1, 3) if s in RELAYED else (1, 3, 2):
            send("h", ("h", s, o), factor.at[s, 0, x, core], factor.at[s, STEPS.index(o), x, core], dzh=o)
        along_x(s, 0)

    def along_x(s, o):
        piece = factor.at[s, STEPS.index(o), x, core]
        part = [o in steps for steps in PARTS].index(True)
        for by in (2, 1, -1):
            send("x", ("x", s, part), piece, piece, dx=by)

    def from_zh(s, o):
        arrive(("h", s, o), factor.at[s, STEPS.index(o), x, core])
        if s in RELAYED and o != 2:
            half = slice(0, WP // 2) if o == 1 else slice(WP // 2, WP)
            source = factor.at[s, STEPS.index(o), x, core, half]
            send("h", ("h", s, 2), source, factor.at[s, STEPS.index(2), x, core, half], dzh=o)
        along_x(s, o)

    def to_core(s, part):
        arrive(("x", s, part), factor.at[s, slots(part), 0 : X - 1, core])
        pieces = factor.at[s, slots(part), :, core]
        send("c", ("c", s, part), pieces, pieces, dcore=1)

    def multiply(s, part):
        arrive(("c", s, part), factor.at[s, slots(part), :, 1 - core])
        count = len(PARTS[part])
        b_high, b_low = split(factor[s, slots(part)].reshape(count * WZ, DEPTH))
        product = dot3(a_high[...], a_low[...], b_high, b_low, ((1,), (1,)))
        for n in range(count):
            columns = product[:, n * WZ : (n + 1) * WZ]
            partial[s, slots(part).start + n] = columns.reshape(ZL, Y, OUT, WZ)
        for at, way, rows in ((0, 1, slice(0, 8)), (1, -1, slice(8, 16))):
            source = partial.at[s, slots(part), :, turn(y, 4, Y), rows]
            send("r", ("r", s, part, 0), source, half_in.at[s, at, slots(part)], dy=way)

    def reduce_y(s, part, step):
        at_part = slots(part)
        if step == 0:
            arrive(("r", s, part, 0), half_in.at[s, :, at_part])
        else:
            arrive(("r", s, part, step), step_in.at[s, step - 1, :, at_part])
        for at, way, rows in ((0, 1, slice(0, 8)), (1, -1, slice(8, 16))):
            if step == 0:
                partial[s, at_part, :, turn(y, 3 * way, Y), rows] += half_in[s, at, at_part]
            else:
                partial[s, at_part, :, turn(y, (3 - step) * way, Y)] += step_in[s, step - 1, at, at_part]
            if step < 3:
                source = partial.at[s, at_part, :, turn(y, (3 - step) * way, Y)]
                send("r", ("r", s, part, step + 1), source, step_in.at[s, step, at, at_part], dy=way)
        if step == 3:
            for o in (1, 2):
                source = partial.at[s, at_part, turn(zl, o, ZL), y]
                send("w", ("w", s, part), source, last_in.at[s, o - 1, at_part], dzl=o)

    def finish(s, part):
        arrive(("w", s, part), last_in.at[s, :, slots(part)])
        for o in PARTS[part]:
            at = STEPS.index(o)
            columns = pl.ds(pl.multiple_of(turn(zh, -o, ZH) * WZ, WZ), WZ)
            total = partial[s, at, zl, y] + (last_in[s, 0, at] + last_in[s, 1, at])
            if s:
                total = total + o_ref[s, :, columns]
            o_ref[s, :, columns] = -total

    def couple(s):
        high, low = split(o_ref[s])
        o_ref[s + 1] = dot3(high, low, k_high[s], k_low[s], ((1,), (0,)))

    def prepare():
        fill_a.wait()
        fill_k.wait()
        a_high[...], a_low[...] = split(a_ref[...])
        k_high[...], k_low[...] = split(k_ref[...])

    events = (
        prepare, gather_y, pick, own, from_zh, to_core, multiply, reduce_y, finish, couple,
    )
    for what, *given in ORDER:
        events[what](*given)
    all_sent("l", from_zl)
    all_sent("h", picked)
    all_sent("x", factor.at[:, :, 0:3, 0])
    all_sent("c", factor.at[:, :, :, 0])
    for s in range(S):
        all_sent(("y", s), listed[s].at[0 : Y - 1])
    all_sent("r", partial.at[:, :, :, 0 : Y - 1])
    all_sent("w", last_in)
    assert (len(sends), len(arrivals)) == (SENDS, ARRIVALS)


def fused(table, inverse_tiles, factor_panels, couplings):
    hbm = pl.BlockSpec(memory_space=pltpu.HBM)
    return pl.pallas_call(
        kernel,
        out_shape=jax.ShapeDtypeStruct((S, OUT, W), F32),
        in_specs=[pl.BlockSpec(memory_space=pltpu.SMEM), hbm, hbm, hbm],
        out_specs=pl.BlockSpec(memory_space=pltpu.VMEM),
        scratch_shapes=[
            pltpu.VMEM((ROWS, DEPTH), F32),
            pltpu.VMEM((S - 1, W, W), F32),
            pltpu.VMEM((S, 2, WP, 128), F32),
            pltpu.VMEM((Y, 2, WP, 128), F32),
            pltpu.VMEM((Y, 2, WP, 128), F32),
            pltpu.VMEM((Y, 2, WP, 128), F32),
            pltpu.VMEM((S, ZL, WP, DEPTH), F32),
            pltpu.VMEM((S, 2, WP, DEPTH), F32),
            pltpu.VMEM((S, ZH, X, CORE, WP, DEPTH), F32),
            pltpu.VMEM((S, ZH, ZL, Y, OUT, WZ), F32),
            pltpu.VMEM((S, 2, ZH, ZL, OUT // 2, WZ), F32),
            pltpu.VMEM((S, 3, 2, ZH, ZL, OUT, WZ), F32),
            pltpu.VMEM((S, 2, ZH, OUT, WZ), F32),
            pltpu.VMEM((ROWS, DEPTH), BF16),
            pltpu.VMEM((ROWS, DEPTH), BF16),
            pltpu.VMEM((S - 1, W, W), BF16),
            pltpu.VMEM((S - 1, W, W), BF16),
            pltpu.SemaphoreType.DMA((4,)),
            pltpu.SemaphoreType.DMA((SENDS,)),
            pltpu.SemaphoreType.DMA((ARRIVALS,)),
        ],
        compiler_params=pltpu.CompilerParams(
            collective_id=0, has_side_effects=True, vmem_limit_bytes=60 * 1024 * 1024
        ),
    )(table, inverse_tiles, factor_panels, couplings)


def on_device(inverse_tiles, factor_panels, block_rows, couplings):
    col = lax.axis_index("col")
    zl, y = col // Y, lax.rem(col, Y)
    target = jnp.arange(TARGETS, dtype=jnp.int32)
    wanted = (target // NBC * Y + y) * NBC + target % NBC
    number = jnp.arange(1, NZB + 1, dtype=jnp.int32)
    found = jnp.sum(
        jnp.where(block_rows[:, None, :] == wanted[:, None], number, 0), axis=2
    )
    local = found - 1 - zl * (Y * LISTED)
    here = (found > 0) & (local >= 0) & (local < Y * LISTED)
    slot = (y + (Y - 1) - local // LISTED) % Y
    code = jnp.where(here, slot * LISTED + local % LISTED, Y * LISTED)
    return fused(code, inverse_tiles, factor_panels, couplings)


def solution(mesh):
    return jax.shard_map(
        on_device,
        mesh=mesh,
        in_specs=(P("row", "col"), P(None, "row", "col"), P(), P()),
        out_specs=P(None, ("row", "col"), None),
        check_vma=False,
    )
```
